32 devices in a mesh: region: 2 (over y), curve: 4 (over z), chain: 2 (over x), rep: 2 (over core).
Axes of the slice: x: 2, y: 2, z: 4, core: 2. Of those that a mesh axis runs over, the one named last changes fastest.
Arguments:
- values: bfloat16 [64, 131072], P('chain', ('region', 'curve', 'rep')), parts along dimension 1, may hold values from -6 to 6
- factor: bfloat16 [2048, 64, 320], P(('region', 'curve', 'rep')), parts along dimension 0
- cond: int32 [2048, 4], P(('region', 'curve', 'rep')), parts along dimension 0, may hold values from -1 to 1023, as said below
- live: int32 [16], P(('region', 'curve', 'rep')), parts along dimension 0, may hold values from 64 to 128, as said below
Outputs:
- gradient: float32 [64, 131072], P('chain', ('region', 'curve', 'rep')), parts along dimension 1
The draws below stay inside these ranges and needn't reach their ends.
There are 2 independent parts, one for each index of `region`. The reference program is written for one: setup_inputs(seed, part) draws one part's arguments, and reference() takes and returns one part's arrays. A program takes and returns all parts, laid end to end along the dimension named above; each array names one. Nothing has to cross between parts.
Inputs may be any that keep to these rules, and one draw needn't show every extreme that they name: Slots below a device's count are live blocks, the rest padding; some device has 128 live blocks and another half of 128. `cond`: A row lists distinct live blocks earlier than its own block, each held by the same device along curve+rep or by one of the two devices before it; -1 marks an empty entry, stands after all others in its row, and appears only where fewer than 4 such blocks exist; rows of padding slots are all -1.
All inputs are finite; a program needn't handle non-finite values.
Results may differ from the reference program's by a relative error of at most 0.0023.
Values may be sent and summed in bfloat16 or wider, within the bound.
No kernel may reach another device: no remote copies, remote signals or barrier semaphores. Data moves between devices by JAX's collectives and lax.ppermute only.
A program may use at most 128 MiB of HBM per device.

```python
import jax
import jax.numpy as jnp
from jax import lax

BS = 64
KN = 4
BLK_CAP = 128
CH = 64
DEVS_CURVE = 8
NBLK = 1024
NROWS = 65536


def plan_live(key):
    draw_key = jax.random.fold_in(key, 17)
    key_a, key_b, key_c = jax.random.split(draw_key, 3)
    counts = jax.random.randint(key_a, (DEVS_CURVE,), BLK_CAP // 2, BLK_CAP + 1)
    full_dev = jax.random.randint(key_b, (), 0, DEVS_CURVE)
    half_dev = (full_dev + jax.random.randint(key_c, (), 1, DEVS_CURVE)) % DEVS_CURVE
    dev_ids = jnp.arange(DEVS_CURVE)
    counts = jnp.where(dev_ids == full_dev, BLK_CAP, counts)
    counts = jnp.where(dev_ids == half_dev, BLK_CAP // 2, counts)
    return counts.astype(jnp.int32)


def draw_live(key, part):
    return plan_live(key)


def draw_cond(key, part):
    counts = plan_live(key)
    block_ids = jnp.arange(NBLK, dtype=jnp.int32)
    owner_dev = block_ids // BLK_CAP
    span = 3 * BLK_CAP
    offsets = jnp.arange(span, dtype=jnp.int32)
    window_ids = (owner_dev[:, None] - 2) * BLK_CAP + offsets[None, :]
    safe_ids = jnp.clip(window_ids, 0, NBLK - 1)
    usable = (window_ids >= 0) & (window_ids < block_ids[:, None])
    usable = usable & (safe_ids % BLK_CAP < counts[safe_ids // BLK_CAP])
    active = block_ids % BLK_CAP < counts[owner_dev]
    usable = usable & active[:, None]
    scores = jax.random.randint(jax.random.fold_in(key, 29), (NBLK, span), 0, 2 ** 20) * span + offsets[None, :]
    scores = jnp.where(usable, scores, -1)
    top_scores, top_pos = lax.top_k(scores, KN)
    chosen = jnp.take_along_axis(window_ids, top_pos, axis=1)
    return jnp.where(top_scores >= 0, chosen, -1).astype(jnp.int32)


def draw_factor(key, part):
    draw_key = jax.random.fold_in(key, 41)
    noise = jax.random.normal(draw_key, (NBLK, BS, BS * (KN + 1)), jnp.float32) * 0.1
    diagonal = (jnp.arange(BS)[:, None] == jnp.arange(BS * (KN + 1))[None, :]).astype(jnp.float32) * 1.5
    matrix = noise + diagonal[None, :, :]
    return matrix.astype(jnp.bfloat16)


def block_levels(key, extent, pieces, least, largest):
    def one(dim, parts):
        steps = jax.random.uniform(jax.random.fold_in(jax.random.fold_in(key, 6), dim), (parts,), jnp.float32, least / len(pieces), largest / len(pieces))
        return jnp.repeat(jnp.exp(steps), extent[dim] // parts).reshape((-1,) + (1,) * (len(extent) - dim - 1))

    level = one(*pieces[0])
    for cut in pieces[1:]:
        level = level * one(*cut)
    return level


def bell_draw(stream_key, shape, scale, bound, cuts=(), kind=jnp.bfloat16):
    entries = jax.random.normal(stream_key, shape, jnp.float32) * scale
    if len(cuts) > 0:
        entries = block_levels(stream_key, shape, cuts, -0.22, 0.18) * entries
    return jnp.clip(entries, min=-bound, max=bound).astype(kind)


def setup_inputs(seed: int = 0, part: int = 0) -> dict:
    arg_keys = jax.random.split(jax.random.key(seed), 5)
    part_splits = jax.random.split(jax.random.fold_in(arg_keys[4], part), 5)
    values = bell_draw(part_splits[0], (CH, NROWS), 1.0, 6.0, ((0, 2), (1, 8)))
    factor = draw_factor(jax.random.fold_in(jax.random.fold_in(arg_keys[4], part), 71), part)
    cond = draw_cond(jax.random.fold_in(jax.random.fold_in(arg_keys[4], part), 71), part)
    live = draw_live(jax.random.fold_in(jax.random.fold_in(arg_keys[4], part), 71), part)
    return {"values": values, "factor": factor, "cond": cond, "live": live}


def reference(values, factor, cond, live):
    value_blocks = values.reshape(CH, NBLK, BS)
    block_ids = jnp.arange(NBLK, dtype=jnp.int32)
    owner_dev = block_ids // BLK_CAP
    active = (block_ids % BLK_CAP) < live[owner_dev]
    present = cond >= 0
    safe_index = jnp.where(present, cond, 0).astype(jnp.int32)
    near_blocks = value_blocks[:, safe_index, :]
    near_blocks = jnp.where(present[None, :, :, None], near_blocks, jnp.zeros_like(near_blocks))
    stacked = jnp.concatenate([value_blocks[:, :, None, :], near_blocks], axis=2).reshape(CH, NBLK, BS * (KN + 1))
    residual = jnp.einsum("bij,cbj->cbi", factor.astype(jnp.float32), stacked.astype(jnp.float32))
    residual = jnp.where(active[None, :, None], residual, jnp.zeros_like(residual)).astype(jnp.bfloat16)
    terms = jnp.einsum("bij,cbi->cbj", factor.astype(jnp.float32), residual.astype(jnp.float32))
    gradient = -terms[:, :, :BS]
    back_terms = terms[:, :, BS:].reshape(CH, NBLK, KN, BS)
    back_terms = jnp.where(present[None, :, :, None], back_terms, jnp.zeros_like(back_terms))
    gradient = gradient.at[:, safe_index].add(-back_terms)
    return gradient.reshape(CH, NROWS)
```

```python
import functools

import jax
import jax.numpy as jnp
from jax import lax
from jax.experimental import pallas as pl
from jax.experimental.pallas import tpu as pltpu
from jax.sharding import PartitionSpec as P

BS = 64
KN = 4
LANES = 128
GROUP = 4
PIECES = 8
CHUNKS = 1


def shift(block, axis, distance):
    size = lax.axis_size(axis)
    return lax.ppermute(
        block, axis, [(i - distance, i) for i in range(size) if 0 <= i - distance < size]
    )


def swap(block):
    return lax.ppermute(block, "rep", [(0, 1), (1, 0)])


def half_roll(tile):
    return jnp.concatenate([tile[..., BS:], tile[..., :BS]], axis=-1)


def kernel(
    first_row, index, live, two, one, own, factor,
    out_two, out_one, out_own,
    held, window, low, high, sems,
):
    chains = two.shape[0]
    blocks = held.shape[0]
    tiles = blocks // 2
    per_piece = blocks // PIECES
    copies = [
        pltpu.make_async_copy(
            factor.at[pl.ds(i * per_piece, per_piece)],
            held.at[pl.ds(i * per_piece, per_piece)],
            sems.at[i],
        )
        for i in range(PIECES)
    ]
    for copy in copies:
        copy.start()

    rows = pl.ds(first_row, chains)
    for region, source in enumerate((two, one, own)):
        source_rows = rows if region == 2 else slice(None)

        def spread(t, carry, region=region, source=source, source_rows=source_rows):
            tile = source[source_rows, pl.ds(pl.multiple_of(t * LANES, LANES), LANES)]
            window[region * blocks + 2 * t] = tile
            window[region * blocks + 2 * t + 1] = half_roll(tile)
            return carry

        lax.fori_loop(0, tiles, spread, 0, unroll=8)
    window[pl.ds(3 * blocks, 2)] = jnp.zeros((2, chains, LANES), window.dtype)

    def clear(i, carry):
        zero = jnp.zeros((8, chains, LANES), jnp.float32)
        low[pl.ds(i * 8, 8)] = zero
        high[pl.ds(i * 8, 8)] = zero
        return carry

    lax.fori_loop(0, 2 * blocks // 8, clear, 0, unroll=2)
    low[pl.ds(3 * blocks, 1)] = jnp.zeros((1, chains, LANES), jnp.float32)
    high[pl.ds(3 * blocks, 1)] = jnp.zeros((1, chains, LANES), jnp.float32)

    in_low = lax.broadcasted_iota(jnp.int32, (chains, LANES), 1) < BS
    shape = (GROUP * chains, GROUP * BS)
    row_block = lax.broadcasted_iota(jnp.int32, shape, 0) // chains
    lane_block = lax.broadcasted_iota(jnp.int32, shape, 1) // BS
    diagonal = row_block == lane_block
    live_count = live[0]

    def group(q, carry):
        first = q * GROUP
        stacked = []
        places = []
        for b in range(GROUP):
            g = first + b
            at = [index[g * KN + k] for k in range(KN)]
            places.append(at)
            stacked.append(
                jnp.concatenate(
                    [
                        jnp.where(in_low, window[2 * blocks + g], window[at[0] ^ 1]),
                        jnp.where(in_low, window[at[1]], window[at[2] ^ 1]),
                        window[at[3]][:, :BS],
                    ],
                    axis=1,
                )
            )
        stacked = jnp.concatenate(stacked, axis=0)
        maps = held[pl.ds(first, GROUP)].reshape(GROUP * BS, BS * (KN + 1))
        residual = lax.dot_general(
            stacked, maps, (((1,), (1,)), ((), ())), preferred_element_type=jnp.float32
        )
        kept = diagonal & (lane_block < live_count - first)
        residual = jnp.where(kept, residual, 0.0).astype(jnp.bfloat16)
        terms = jnp.dot(residual, maps, preferred_element_type=jnp.float32)
        for b in range(GROUP):
            g = first + b
            at = places[b]
            t0 = terms[b * chains : (b + 1) * chains, :LANES]
            t1 = terms[b * chains : (b + 1) * chains, LANES : 2 * LANES]
            t2 = terms[b * chains : (b + 1) * chains, 2 * LANES :]
            t2 = jnp.concatenate([t2, t2], axis=1)
            u0, l1, u2, l3 = high[at[0]], low[at[1]], high[at[2]], low[at[3]]
            high[at[0]] = u0 + t0
            low[at[1]] = l1 + t1
            high[at[2]] = u2 + t1
            low[at[3]] = l3 + t2
            low[2 * blocks + g] = t0
            high[2 * blocks + g] = jnp.zeros_like(t0)
        return carry

    for i, copy in enumerate(copies):
        copy.wait()
        lax.fori_loop(i * per_piece // GROUP, (i + 1) * per_piece // GROUP, group, 0)

    for region, target in enumerate((out_two, out_one, out_own)):

        def gather(t, carry, region=region, target=target):
            even = region * blocks + 2 * t
            straight = jnp.where(in_low, low[even], high[even + 1])
            crossed = jnp.where(in_low, low[even + 1], high[even])
            total = -(straight + half_roll(crossed))
            target[:, pl.ds(pl.multiple_of(t * LANES, LANES), LANES)] = total.astype(target.dtype)
            return carry

        lax.fori_loop(0, tiles, gather, 0, unroll=8)


def local_terms(first_row, index, live, two, one, own, factor):
    chains, row_count = two.shape
    blocks = factor.shape[0]
    width = factor.shape[2]
    vmem = pl.BlockSpec(memory_space=pltpu.VMEM)
    smem = pl.BlockSpec(memory_space=pltpu.SMEM)
    slots = 3 * blocks + 2
    return pl.pallas_call(
        functools.partial(kernel, first_row),
        out_shape=(
            jax.ShapeDtypeStruct((chains, row_count), jnp.bfloat16),
            jax.ShapeDtypeStruct((chains, row_count), jnp.float32),
            jax.ShapeDtypeStruct((chains, row_count), jnp.float32),
        ),
        in_specs=[smem, smem, vmem, vmem, vmem, pl.BlockSpec(memory_space=pl.ANY)],
        out_specs=(vmem, vmem, vmem),
        scratch_shapes=[
            pltpu.VMEM((blocks, BS, width), jnp.bfloat16),
            pltpu.VMEM((slots, chains, LANES), jnp.bfloat16),
            pltpu.VMEM((slots, chains, LANES), jnp.float32),
            pltpu.VMEM((slots, chains, LANES), jnp.float32),
            pltpu.SemaphoreType.DMA((PIECES,)),
        ],
        compiler_params=pltpu.CompilerParams(vmem_limit_bytes=44 * 2**20),
        cost_estimate=pl.CostEstimate(
            flops=16 * blocks * BS * width * chains, bytes_accessed=8 * 2**20, transcendentals=0
        ),
    )(index, live, two, one, own, factor)


def body(values, factor, cond, live):
    chains, row_count = values.shape
    blocks = factor.shape[0]
    position = lax.axis_index(("curve", "rep"))
    core = lax.axis_index("rep")
    index = jnp.where(cond >= 0, cond - (position - 2) * blocks, 3 * blocks).reshape(-1)
    part = chains // CHUNKS
    arrived = [
        shift(values[c * part : (c + 1) * part], "curve", 1) for c in range(CHUNKS)
    ]
    results = []
    for c in range(CHUNKS):
        own = values[c * part : (c + 1) * part]
        one = swap(jnp.where(core == 0, own, arrived[c]))
        to_two, to_one, mine = local_terms(c * part, index, live, arrived[c], one, values, factor)
        across = swap(to_one)
        to_two = to_two.astype(jnp.float32) + jnp.where(core == 1, across, jnp.zeros_like(across))
        back = shift(to_two.astype(jnp.bfloat16), "curve", -1)
        results.append(
            mine + jnp.where(core == 0, across, jnp.zeros_like(across)) + back.astype(jnp.float32)
        )
    return jnp.concatenate(results, axis=0)


def solution(mesh):
    placed = (
        P("chain", ("region", "curve", "rep")),
        P(("region", "curve", "rep"), None, None),
        P(("region", "curve", "rep"), None),
        P(("region", "curve", "rep")),
    )
    return jax.shard_map(
        body,
        mesh=mesh,
        in_specs=placed,
        out_specs=P("chain", ("region", "curve", "rep")),
        check_vma=False,
    )
```

```python
import jax
import jax.numpy as jnp
from jax import lax
from jax.experimental import pallas as pl
from jax.experimental.pallas import tpu as pltpu
from jax.sharding import PartitionSpec as P

BS = 64
KN = 4
LANES = 128
GROUP = 4
UNROLL = 16
PIECES = 4

VMEM = pl.BlockSpec(memory_space=pltpu.VMEM)
SMEM = pl.BlockSpec(memory_space=pltpu.SMEM)
HBM = pl.BlockSpec(memory_space=pltpu.HBM)


def to_next_chip(block, core):
    size = lax.axis_size("curve")
    return lax.ppermute(
        block, ("curve", "rep"), [(2 * z + core, 2 * z + 2 + core) for z in range(size - 1)]
    )


def from_next_chip(block, core):
    size = lax.axis_size("curve")
    return lax.ppermute(
        block, ("curve", "rep"), [(2 * z + 2 + core, 2 * z + core) for z in range(size - 1)]
    )


def swap(block):
    return lax.ppermute(block, "rep", [(0, 1), (1, 0)])


def half_roll(tile):
    return pltpu.roll(tile, BS, tile.ndim - 1)


def lane_tile(t):
    return pl.ds(pl.multiple_of(t * LANES, LANES), LANES)


def low_lanes(rows):
    return lax.broadcasted_iota(jnp.int32, (rows, LANES), 1) < BS


def cross(low, first, second):
    kept = jnp.where(low, first, second)
    moved = half_roll(jnp.where(low, second, first))
    return jnp.where(low, kept, moved), jnp.where(low, moved, kept)


def spread(source, window, first_block):
    def step(t, carry):
        tile = source[:, lane_tile(t)]
        window[first_block + 2 * t] = tile
        window[first_block + 2 * t + 1] = half_roll(tile.astype(jnp.float32)).astype(tile.dtype)
        return carry

    lax.fori_loop(0, source.shape[1] // LANES, step, 0, unroll=8)


def collect(total, first_block, target):
    low = low_lanes(total.shape[1])

    def step(t, carry):
        even = first_block + 2 * t
        upper, lower = cross(low, total[even], total[even + 1])
        tile = jnp.concatenate([upper, lower], axis=0).astype(target.dtype)
        target[:, lane_tile(t)] = tile
        return carry

    lax.fori_loop(0, target.shape[1] // LANES, step, 0, unroll=8)


def turn_kernel(flipped, factor, staged, sems):
    pieces = staged.shape[0]
    rows = staged.shape[1]
    copies = [
        pltpu.make_async_copy(flipped.at[pl.ds(i * rows, rows)], staged.at[i], sems.at[i])
        for i in range(pieces)
    ]
    for copy in copies:
        copy.start()
    for i, copy in enumerate(copies):
        copy.wait()
        factor[:, pl.ds(i * rows, rows), :] = jnp.transpose(staged[i], (2, 0, 1))


def payload_kernel(core, own, arrived, factor, index, target):
    @pl.when(core[0] == 0)
    def _():
        target[...] = own[...]

    @pl.when(core[0] != 0)
    def _():
        target[...] = arrived[...]


def own_kernel(own, index, window, total, again):
    again[...] = own[...]
    blocks = own.shape[1] // BS
    half = total.shape[1]
    spread(own, window, 2 * blocks)
    window[pl.ds(3 * blocks, 2)] = jnp.zeros((2,) + window.shape[1:], window.dtype)

    def clear(i, carry):
        total[pl.ds(i * 8, 8)] = jnp.zeros((8, half, LANES), jnp.float32)
        return carry

    lax.fori_loop(0, 2 * blocks // 8, clear, 0, unroll=4)
    total[3 * blocks] = jnp.zeros((half, LANES), jnp.float32)


def halo_kernel(core, one, two_even, two_odd, window_in, window):
    spread(one, window, one.shape[1] // BS)

    @pl.when(core[0] == 0)
    def _():
        spread(two_even, window, 0)

    @pl.when(core[0] != 0)
    def _():
        spread(two_odd, window, 0)


def main_kernel(
    index, live, window, total_in, factor, out_one, total, residuals,
):
    chains = window.shape[1]
    half = chains // 2
    blocks = factor.shape[0]

    low = low_lanes(chains)
    half_low = low_lanes(half)
    shape = (GROUP * chains, GROUP * BS)
    row_block = lax.broadcasted_iota(jnp.int32, shape, 0) // chains
    lane_block = lax.broadcasted_iota(jnp.int32, shape, 1) // BS
    diagonal = row_block == lane_block
    live_count = live[0]

    def pull(q, carry):
        first = q * GROUP
        stacked = []
        for b in range(GROUP):
            g = first + b
            at = [index[g * KN + k] for k in range(KN)]
            stacked.append(
                jnp.concatenate(
                    [
                        jnp.where(low, window[2 * blocks + g], window[at[0] ^ 1]),
                        jnp.where(low, window[at[1]], window[at[2] ^ 1]),
                        window[at[3]][:, :BS],
                    ],
                    axis=1,
                )
            )
        stacked = jnp.concatenate(stacked, axis=0)
        maps = factor[pl.ds(first, GROUP)].reshape(GROUP * BS, BS * (KN + 1))
        residual = lax.dot_general(
            stacked, maps, (((1,), (1,)), ((), ())), preferred_element_type=jnp.float32
        )
        kept = diagonal & (lane_block < live_count - first)
        residuals[q] = jnp.where(kept, -residual, 0.0).astype(jnp.bfloat16)
        return carry

    def push(q, carry):
        first = q * GROUP
        maps = factor[pl.ds(first, GROUP)].reshape(GROUP * BS, BS * (KN + 1))
        terms = jnp.dot(residuals[q], maps, preferred_element_type=jnp.float32)
        for b in range(GROUP):
            g = first + b
            at = [index[g * KN + k] for k in range(KN)]
            a = terms[b * chains : b * chains + half]
            z = terms[b * chains + half : (b + 1) * chains]
            mine, t0 = cross(half_low, a[:, :LANES], z[:, :LANES])
            t1, t2 = cross(half_low, a[:, LANES : 2 * LANES], z[:, LANES : 2 * LANES])
            t3 = jnp.concatenate([a[:, 2 * LANES :], z[:, 2 * LANES :]], axis=1)
            old = [total[at[k]] for k in range(KN)]
            for k, term in enumerate((t0, t1, t2, t3)):
                total[at[k]] = old[k] + term
            total[2 * blocks + g] = mine
        return carry

    lax.fori_loop(0, blocks // GROUP, pull, 0, unroll=UNROLL)
    lax.fori_loop(0, blocks // GROUP, push, 0, unroll=UNROLL)
    collect(total, blocks, out_one)


def add_across(core, keeper, total, across, target, first_block):
    low = low_lanes(total.shape[1])
    share = jnp.where(core[0] == keeper, 1.0, 0.0)

    def step(t, carry):
        even = first_block + 2 * t
        upper, lower = cross(low, total[even], total[even + 1])
        tile = jnp.concatenate([upper, lower], axis=0) + share * across[:, lane_tile(t)]
        target[:, lane_tile(t)] = tile.astype(target.dtype)
        return carry

    lax.fori_loop(0, target.shape[1] // LANES, step, 0, unroll=8)


def two_kernel(total, target):
    collect(total, 0, target)


def joint_kernel(core, total, across, target):
    add_across(core, 1, total, across, target, 0)


def mine_kernel(core, total, across, target):
    add_across(core, 0, total, across, target, 2 * (target.shape[1] // BS))


def call(kernel, outs, specs, args, out_specs=VMEM, **more):
    return pl.pallas_call(
        kernel,
        out_shape=outs,
        in_specs=specs,
        out_specs=out_specs,
        **more,
    )(*args)


LITTLE = pl.CostEstimate(flops=0, bytes_accessed=1024, transcendentals=0)


def params(mib):
    return pltpu.CompilerParams(vmem_limit_bytes=mib * 2**20)


def body(values, factor, cond, live):
    chains, row_count = values.shape
    blocks, rows, width = factor.shape
    slots = 3 * blocks + 2
    position = lax.axis_index(("curve", "rep"))
    core = lax.axis_index("rep").reshape(1)
    index = jnp.where(cond >= 0, cond - (position - 2) * blocks, 3 * blocks).reshape(-1)
    narrow = jax.ShapeDtypeStruct((chains, row_count), jnp.bfloat16)
    wide = jax.ShapeDtypeStruct((chains, row_count), jnp.float32)
    window_shape = jax.ShapeDtypeStruct((slots, chains, LANES), jnp.bfloat16)
    total_shape = jax.ShapeDtypeStruct((slots, chains // 2, LANES), jnp.float32)

    two_odd = to_next_chip(values, 1)
    window, total, again = call(
        own_kernel,
        (window_shape, total_shape, narrow),
        [VMEM, SMEM],
        (values, index),
        out_specs=(VMEM, VMEM, VMEM),
        compiler_params=params(4),
        cost_estimate=LITTLE,
    )
    two_even = to_next_chip(again, 0)
    factor = call(
        turn_kernel,
        jax.ShapeDtypeStruct(factor.shape, factor.dtype),
        [HBM],
        (jnp.transpose(factor, (1, 2, 0)),),
        scratch_shapes=[
            pltpu.VMEM((PIECES, rows // PIECES, width, blocks), factor.dtype),
            pltpu.SemaphoreType.DMA((PIECES,)),
        ],
        compiler_params=params(16),
        cost_estimate=pl.CostEstimate(flops=0, bytes_accessed=14 * 2**20, transcendentals=0),
    )
    payload = call(
        payload_kernel,
        narrow,
        [SMEM, VMEM, VMEM, VMEM, SMEM],
        (core, values, two_odd, factor, index),
        compiler_params=params(4), cost_estimate=LITTLE,
    )
    one = swap(payload)
    window = call(
        halo_kernel,
        window_shape,
        [SMEM, VMEM, VMEM, VMEM, VMEM],
        (core, one, two_even, two_odd, window),
        input_output_aliases={4: 0}, compiler_params=params(4), cost_estimate=LITTLE
    )
    to_one, total = call(
        main_kernel,
        (wide, total_shape),
        [SMEM, SMEM, VMEM, VMEM, VMEM],
        (index, live, window, total, factor),
        out_specs=(VMEM, VMEM),
        scratch_shapes=[
            pltpu.VMEM((blocks // GROUP, GROUP * chains, GROUP * BS), jnp.bfloat16),
        ],
        input_output_aliases={3: 1},
        compiler_params=params(12),
        cost_estimate=pl.CostEstimate(
            flops=16 * blocks * rows * width * chains,
            bytes_accessed=8 * 2**20,
            transcendentals=0,
        ),
    )
    across = swap(to_one)
    to_two = call(two_kernel, narrow, [VMEM], (total,), compiler_params=params(4), cost_estimate=LITTLE)
    back = from_next_chip(to_two, 0)
    joint = call(joint_kernel, narrow, [SMEM, VMEM, VMEM], (core, total, across), compiler_params=params(4), cost_estimate=LITTLE)
    joint = from_next_chip(joint, 1)
    mine = call(mine_kernel, wide, [SMEM, VMEM, VMEM], (core, total, across), compiler_params=params(4), cost_estimate=LITTLE)
    return mine + jnp.where(core == 0, back, joint).astype(jnp.float32)


def solution(mesh):
    placed = (
        P("chain", ("region", "curve", "rep")),
        P(("region", "curve", "rep"), None, None),
        P(("region", "curve", "rep"), None),
        P(("region", "curve", "rep")),
    )
    return jax.shard_map(
        body,
        mesh=mesh,
        in_specs=placed,
        out_specs=P("chain", ("region", "curve", "rep")),
        check_vma=False,
    )
```

```python
import jax
import jax.numpy as jnp
from jax import lax
from jax.experimental import pallas as pl
from jax.experimental.pallas import tpu as pltpu
from jax.sharding import PartitionSpec as P

BS = 64
KN = 4
LANES = 128
GROUP = 4
UNROLL = 16
PIECES = 4
SETUP_MIB = 12

VMEM = pl.BlockSpec(memory_space=pltpu.VMEM)
SMEM = pl.BlockSpec(memory_space=pltpu.SMEM)
HBM = pl.BlockSpec(memory_space=pltpu.HBM)


def to_next_chip(block, core):
    size = lax.axis_size("curve")
    return lax.ppermute(
        block, ("curve", "rep"), [(2 * z + core, 2 * z + 2 + core) for z in range(size - 1)]
    )


def from_next_chip(block, core):
    size = lax.axis_size("curve")
    return lax.ppermute(
        block, ("curve", "rep"), [(2 * z + 2 + core, 2 * z + core) for z in range(size - 1)]
    )


def swap(block):
    return lax.ppermute(block, "rep", [(0, 1), (1, 0)])


def half_roll(tile):
    return pltpu.roll(tile, BS, tile.ndim - 1)


def lane_tile(t):
    return pl.ds(pl.multiple_of(t * LANES, LANES), LANES)


def low_lanes(rows):
    return lax.broadcasted_iota(jnp.int32, (rows, LANES), 1) < BS


def cross(low, first, second):
    kept = jnp.where(low, first, second)
    moved = half_roll(jnp.where(low, second, first))
    return jnp.where(low, kept, moved), jnp.where(low, moved, kept)


def spread(source, window, first_block):
    def step(t, carry):
        tile = source[:, lane_tile(t)]
        window[first_block + 2 * t] = tile
        window[first_block + 2 * t + 1] = half_roll(tile.astype(jnp.float32)).astype(tile.dtype)
        return carry

    lax.fori_loop(0, source.shape[1] // LANES, step, 0, unroll=32)


def collect(total, first_block, target):
    low = low_lanes(total.shape[1])

    def step(t, carry):
        even = first_block + 2 * t
        upper, lower = cross(low, total[even], total[even + 1])
        tile = jnp.concatenate([upper, lower], axis=0).astype(target.dtype)
        target[:, lane_tile(t)] = tile
        return carry

    lax.fori_loop(0, target.shape[1] // LANES, step, 0, unroll=32)


def again_kernel(own, index, again, sem):
    copy = pltpu.make_async_copy(own, again, sem)
    copy.start()
    copy.wait()


def setup_kernel(own, flipped, window, total, factor, staged, sems):
    pieces, rows = staged.shape[:2]
    blocks = factor.shape[0]
    half = total.shape[1]
    copies = [
        pltpu.make_async_copy(flipped.at[pl.ds(i * rows, rows)], staged.at[i], sems.at[i])
        for i in range(pieces)
    ]
    for copy in copies:
        copy.start()
    spread(own, window, 2 * blocks)
    window[pl.ds(3 * blocks, 2)] = jnp.zeros((2,) + window.shape[1:], window.dtype)

    def clear(i, carry):
        total[pl.ds(i * 8, 8)] = jnp.zeros((8, half, LANES), jnp.float32)
        return carry

    lax.fori_loop(0, 2 * blocks // 8, clear, 0, unroll=4)
    total[3 * blocks] = jnp.zeros((half, LANES), jnp.float32)
    for i, copy in enumerate(copies):
        copy.wait()
        factor[:, pl.ds(i * rows, rows), :] = jnp.transpose(staged[i], (2, 0, 1))


def payload_kernel(core, own, arrived, factor, index, target):
    @pl.when(core[0] == 0)
    def _():
        target[...] = own[...]

    @pl.when(core[0] != 0)
    def _():
        target[...] = arrived[...]


def halo_kernel(core, one, two_even, two_odd, window_in, window):
    spread(one, window, one.shape[1] // BS)

    @pl.when(core[0] == 0)
    def _():
        spread(two_even, window, 0)

    @pl.when(core[0] != 0)
    def _():
        spread(two_odd, window, 0)


def main_kernel(
    index, live, window, total_in, factor, out_one, total, residuals,
):
    chains = window.shape[1]
    half = chains // 2
    blocks = factor.shape[0]

    low = low_lanes(chains)
    half_low = low_lanes(half)
    shape = (GROUP * chains, GROUP * BS)
    row_block = lax.broadcasted_iota(jnp.int32, shape, 0) // chains
    lane_block = lax.broadcasted_iota(jnp.int32, shape, 1) // BS
    diagonal = row_block == lane_block
    live_count = live[0]

    def pull(q, carry):
        first = q * GROUP
        stacked = []
        for b in range(GROUP):
            g = first + b
            at = [index[g * KN + k] for k in range(KN)]
            stacked.append(
                jnp.concatenate(
                    [
                        jnp.where(low, window[2 * blocks + g], window[at[0] ^ 1]),
                        jnp.where(low, window[at[1]], window[at[2] ^ 1]),
                        window[at[3]][:, :BS],
                    ],
                    axis=1,
                )
            )
        stacked = jnp.concatenate(stacked, axis=0)
        maps = factor[pl.ds(first, GROUP)].reshape(GROUP * BS, BS * (KN + 1))
        residual = lax.dot_general(
            stacked, maps, (((1,), (1,)), ((), ())), preferred_element_type=jnp.float32
        )
        kept = diagonal & (lane_block < live_count - first)
        residuals[q] = jnp.where(kept, -residual, 0.0).astype(jnp.bfloat16)
        return carry

    def push(q, carry):
        first = q * GROUP
        maps = factor[pl.ds(first, GROUP)].reshape(GROUP * BS, BS * (KN + 1))
        terms = jnp.dot(residuals[q], maps, preferred_element_type=jnp.float32)
        for b in range(GROUP):
            g = first + b
            at = [index[g * KN + k] for k in range(KN)]
            a = terms[b * chains : b * chains + half]
            z = terms[b * chains + half : (b + 1) * chains]
            mine, t0 = cross(half_low, a[:, :LANES], z[:, :LANES])
            t1, t2 = cross(half_low, a[:, LANES : 2 * LANES], z[:, LANES : 2 * LANES])
            t3 = jnp.concatenate([a[:, 2 * LANES :], z[:, 2 * LANES :]], axis=1)
            old = [total[at[k]] for k in range(KN)]
            for k, term in enumerate((t0, t1, t2, t3)):
                total[at[k]] = old[k] + term
            total[2 * blocks + g] = mine
        return carry

    lax.fori_loop(0, blocks // GROUP, pull, 0, unroll=UNROLL)
    lax.fori_loop(0, blocks // GROUP, push, 0, unroll=UNROLL)
    collect(total, blocks, out_one)


def add_across(core, keeper, total, across, target, first_block):
    low = low_lanes(total.shape[1])
    share = jnp.where(core[0] == keeper, 1.0, 0.0)

    def step(t, carry):
        even = first_block + 2 * t
        upper, lower = cross(low, total[even], total[even + 1])
        tile = jnp.concatenate([upper, lower], axis=0) + share * across[:, lane_tile(t)]
        target[:, lane_tile(t)] = tile.astype(target.dtype)
        return carry

    lax.fori_loop(0, target.shape[1] // LANES, step, 0, unroll=32)


def two_kernel(total, target):
    collect(total, 0, target)


def joint_kernel(core, total, across, target):
    add_across(core, 1, total, across, target, 0)


def mine_kernel(core, total, across, target):
    add_across(core, 0, total, across, target, 2 * (target.shape[1] // BS))


def call(kernel, outs, specs, args, out_specs=VMEM, **more):
    return pl.pallas_call(
        kernel,
        out_shape=outs,
        in_specs=specs,
        out_specs=out_specs,
        **more,
    )(*args)


LITTLE = pl.CostEstimate(flops=0, bytes_accessed=1024, transcendentals=0)


def in_hbm(array):
    return pltpu.with_memory_space_constraint(array, pltpu.HBM)


def params(mib):
    return pltpu.CompilerParams(vmem_limit_bytes=mib * 2**20)


def body(values, factor, cond, live):
    chains, row_count = values.shape
    blocks, rows, width = factor.shape
    slots = 3 * blocks + 2
    position = lax.axis_index(("curve", "rep"))
    core = lax.axis_index("rep").reshape(1)
    index = jnp.where(cond >= 0, cond - (position - 2) * blocks, 3 * blocks).reshape(-1)
    narrow = jax.ShapeDtypeStruct((chains, row_count), jnp.bfloat16)
    wide = jax.ShapeDtypeStruct((chains, row_count), jnp.float32)
    window_shape = jax.ShapeDtypeStruct((slots, chains, LANES), jnp.bfloat16)
    total_shape = jax.ShapeDtypeStruct((slots, chains // 2, LANES), jnp.float32)

    two_odd = to_next_chip(values, 1)
    again = call(
        again_kernel,
        narrow,
        [HBM, SMEM],
        (in_hbm(values), index),
        scratch_shapes=[pltpu.SemaphoreType.DMA],
        compiler_params=params(4),
        cost_estimate=LITTLE,
    )
    two_even = to_next_chip(again, 0)
    window, total, factor = call(
        setup_kernel,
        (window_shape, total_shape, jax.ShapeDtypeStruct(factor.shape, factor.dtype)),
        [VMEM, HBM],
        (again, in_hbm(jnp.transpose(factor, (1, 2, 0)))),
        out_specs=(VMEM, VMEM, VMEM),
        scratch_shapes=[
            pltpu.VMEM((PIECES, rows // PIECES, width, blocks), factor.dtype),
            pltpu.SemaphoreType.DMA((PIECES,)),
        ],
        compiler_params=params(SETUP_MIB),
        cost_estimate=pl.CostEstimate(flops=0, bytes_accessed=14 * 2**20, transcendentals=0),
    )
    payload = call(
        payload_kernel,
        narrow,
        [SMEM, VMEM, VMEM, VMEM, SMEM],
        (core, again, two_odd, factor, index),
        compiler_params=params(4), cost_estimate=LITTLE,
    )
    one = swap(payload)
    window = call(
        halo_kernel,
        window_shape,
        [SMEM, VMEM, VMEM, VMEM, VMEM],
        (core, one, two_even, two_odd, window),
        input_output_aliases={4: 0}, compiler_params=params(4), cost_estimate=LITTLE
    )
    to_one, total = call(
        main_kernel,
        (wide, total_shape),
        [SMEM, SMEM, VMEM, VMEM, VMEM],
        (index, live, window, total, factor),
        out_specs=(VMEM, VMEM),
        scratch_shapes=[
            pltpu.VMEM((blocks // GROUP, GROUP * chains, GROUP * BS), jnp.bfloat16),
        ],
        input_output_aliases={3: 1},
        compiler_params=params(12),
        cost_estimate=pl.CostEstimate(
            flops=16 * blocks * rows * width * chains,
            bytes_accessed=8 * 2**20,
            transcendentals=0,
        ),
    )
    across = swap(to_one)
    to_two = call(two_kernel, narrow, [VMEM], (total,), compiler_params=params(4), cost_estimate=LITTLE)
    back = from_next_chip(to_two, 0)
    joint = call(joint_kernel, narrow, [SMEM, VMEM, VMEM], (core, total, across), compiler_params=params(4), cost_estimate=LITTLE)
    joint = from_next_chip(joint, 1)
    mine = call(mine_kernel, wide, [SMEM, VMEM, VMEM], (core, total, across), compiler_params=params(4), cost_estimate=LITTLE)
    return mine + jnp.where(core == 0, back, joint).astype(jnp.float32)


def solution(mesh):
    placed = (
        P("chain", ("region", "curve", "rep")),
        P(("region", "curve", "rep"), None, None),
        P(("region", "curve", "rep"), None),
        P(("region", "curve", "rep")),
    )
    return jax.shard_map(
        body,
        mesh=mesh,
        in_specs=placed,
        out_specs=P("chain", ("region", "curve", "rep")),
        check_vma=False,
    )
```

```python
import jax
import jax.numpy as jnp
from jax import lax
from jax.experimental import pallas as pl
from jax.experimental.pallas import tpu as pltpu
from jax.sharding import PartitionSpec as P

BS = 64
KN = 4
LANES = 128
GROUP = 4
UNROLL = 16
PIECES = 4
SETUP_MIB = 12

VMEM = pl.BlockSpec(memory_space=pltpu.VMEM)
SMEM = pl.BlockSpec(memory_space=pltpu.SMEM)
HBM = pl.BlockSpec(memory_space=pltpu.HBM)


def to_next_chip(block, core):
    size = lax.axis_size("curve")
    return lax.ppermute(
        block, ("curve", "rep"), [(2 * z + core, 2 * z + 2 + core) for z in range(size - 1)]
    )


def from_next_chip(block, core):
    size = lax.axis_size("curve")
    return lax.ppermute(
        block, ("curve", "rep"), [(2 * z + 2 + core, 2 * z + core) for z in range(size - 1)]
    )


def swap(block):
    return lax.ppermute(block, "rep", [(0, 1), (1, 0)])


def half_roll(tile):
    return pltpu.roll(tile, BS, tile.ndim - 1)


def lane_tile(t):
    return pl.ds(pl.multiple_of(t * LANES, LANES), LANES)


def low_lanes(rows):
    return lax.broadcasted_iota(jnp.int32, (rows, LANES), 1) < BS


def cross(low, first, second):
    kept = jnp.where(low, first, second)
    moved = half_roll(jnp.where(low, second, first))
    return jnp.where(low, kept, moved), jnp.where(low, moved, kept)


def spread(source, window, first_block):
    def step(t, carry):
        tile = source[:, lane_tile(t)]
        window[first_block + 2 * t] = tile
        window[first_block + 2 * t + 1] = half_roll(tile.astype(jnp.float32)).astype(tile.dtype)
        return carry

    lax.fori_loop(0, source.shape[1] // LANES, step, 0, unroll=32)


def collect(total, first_block, target):
    low = low_lanes(total.shape[1])

    def step(t, carry):
        even = first_block + 2 * t
        upper, lower = cross(low, total[even], total[even + 1])
        tile = jnp.concatenate([upper, lower], axis=0).astype(target.dtype)
        target[:, lane_tile(t)] = tile
        return carry

    lax.fori_loop(0, target.shape[1] // LANES, step, 0, unroll=32)


def again_kernel(own, base, core, again, sem):
    copy = pltpu.make_async_copy(own, again, sem)
    copy.start()
    copy.wait()


def setup_kernel(own, flipped, window, total, own_map, near_map, own_part, staged, sems):
    pieces, rows = staged.shape[:2]
    blocks = near_map.shape[0]
    half = total.shape[1]
    copies = [
        pltpu.make_async_copy(flipped.at[pl.ds(i * rows, rows)], staged.at[i], sems.at[i])
        for i in range(pieces)
    ]
    for copy in copies:
        copy.start()
    spread(own, window, 2 * blocks)
    window[pl.ds(3 * blocks, 2)] = jnp.zeros((2,) + window.shape[1:], window.dtype)

    def clear(i, carry):
        total[pl.ds(i * 8, 8)] = jnp.zeros((8, half, LANES), jnp.float32)
        return carry

    lax.fori_loop(0, 3 * blocks // 8, clear, 0, unroll=4)
    total[3 * blocks] = jnp.zeros((half, LANES), jnp.float32)
    for i, copy in enumerate(copies):
        copy.wait()
        part = pl.ds(i * rows, rows)
        own_map[:, part, :] = jnp.transpose(staged[i, :, :BS], (2, 0, 1))
        near_map[:, part, :] = jnp.transpose(staged[i, :, BS:], (2, 0, 1))

    def start(q, carry):
        first = q * GROUP
        mine = [window[2 * blocks + first + b][:, :BS] for b in range(GROUP)]
        maps = own_map[pl.ds(first, GROUP)].reshape(GROUP * BS, BS)
        own_part[q] = lax.dot_general(
            jnp.concatenate(mine, axis=0),
            maps,
            (((1,), (1,)), ((), ())),
            preferred_element_type=jnp.float32,
        )
        return carry

    lax.fori_loop(0, blocks // GROUP, start, 0, unroll=8)


def payload_kernel(core, own, arrived, factor, target):
    @pl.when(core[0] == 0)
    def _():
        target[...] = own[...]

    @pl.when(core[0] != 0)
    def _():
        target[...] = arrived[...]


def main_kernel(
    core, base, cond, live, one, two_even, two_odd, window_in, total_in, near_map, own_part,
    out_one, window, total, residuals, index,
):
    chains = window.shape[1]
    half = chains // 2
    blocks = near_map.shape[0]

    spread(one, window, blocks)

    @pl.when(core[0] == 0)
    def _():
        spread(two_even, window, 0)

    @pl.when(core[0] != 0)
    def _():
        spread(two_odd, window, 0)

    low = low_lanes(chains)
    half_low = low_lanes(half)
    shape = (GROUP * chains, GROUP * BS)
    row_block = lax.broadcasted_iota(jnp.int32, shape, 0) // chains
    lane_block = lax.broadcasted_iota(jnp.int32, shape, 1) // BS
    diagonal = row_block == lane_block
    live_count = live[0]

    def pull(q, carry):
        first = q * GROUP
        stacked = []
        for b in range(GROUP):
            g = first + b
            at = []
            for k in range(KN):
                place = cond[k, g]
                place = jnp.where(place >= 0, place - base[0], 3 * blocks)
                index[g * KN + k] = place
                at.append(place)
            stacked.append(
                jnp.concatenate(
                    [
                        jnp.where(low, window[at[0]], window[at[1] ^ 1]),
                        jnp.where(low, window[at[2]], window[at[3] ^ 1]),
                    ],
                    axis=1,
                )
            )
        stacked = jnp.concatenate(stacked, axis=0)
        maps = near_map[pl.ds(first, GROUP)].reshape(GROUP * BS, BS * KN)
        residual = lax.dot_general(
            stacked, maps, (((1,), (1,)), ((), ())), preferred_element_type=jnp.float32
        )
        residual = residual + own_part[q]
        kept = diagonal & (lane_block < live_count - first)
        residuals[q] = jnp.where(kept, -residual, 0.0).astype(jnp.bfloat16)
        return carry

    def push(q, carry):
        first = q * GROUP
        maps = near_map[pl.ds(first, GROUP)].reshape(GROUP * BS, BS * KN)
        terms = jnp.dot(residuals[q], maps, preferred_element_type=jnp.float32)
        for b in range(GROUP):
            g = first + b
            at = [index[g * KN + k] for k in range(KN)]
            a = terms[b * chains : b * chains + half]
            z = terms[b * chains + half : (b + 1) * chains]
            t0, t1 = cross(half_low, a[:, :LANES], z[:, :LANES])
            t2, t3 = cross(half_low, a[:, LANES:], z[:, LANES:])
            old = [total[at[k]] for k in range(KN)]
            for k, term in enumerate((t0, t1, t2, t3)):
                total[at[k]] = old[k] + term
        return carry

    lax.fori_loop(0, blocks // GROUP, pull, 0, unroll=UNROLL)
    lax.fori_loop(0, blocks // GROUP, push, 0, unroll=UNROLL)
    collect(total, blocks, out_one)


def add_across(core, keeper, total, across, target, first_block):
    low = low_lanes(total.shape[1])
    share = jnp.where(core[0] == keeper, 1.0, 0.0)

    def step(t, carry):
        even = first_block + 2 * t
        upper, lower = cross(low, total[even], total[even + 1])
        tile = jnp.concatenate([upper, lower], axis=0)
        tile = tile + share * across[:, lane_tile(t)].astype(jnp.float32)
        target[:, lane_tile(t)] = tile.astype(target.dtype)
        return carry

    lax.fori_loop(0, target.shape[1] // LANES, step, 0, unroll=32)


def two_kernel(total, target):
    collect(total, 0, target)


def joint_kernel(core, total, across, target):
    add_across(core, 1, total, across, target, 0)


def mine_kernel(core, total, across, residuals, own_map, target, summed):
    blocks = own_map.shape[0]
    chains = target.shape[0]
    half = chains // 2

    def step(q, carry):
        first = q * GROUP
        maps = own_map[pl.ds(first, GROUP)].reshape(GROUP * BS, BS)
        terms = jnp.dot(residuals[q], maps, preferred_element_type=jnp.float32)
        for b in range(GROUP):
            a = terms[b * chains : b * chains + half]
            z = terms[b * chains + half : (b + 1) * chains]
            packed = jnp.concatenate([a, z], axis=1)
            summed[first + b] = total[2 * blocks + first + b] + packed
        return carry

    lax.fori_loop(0, blocks // GROUP, step, 0, unroll=4)
    add_across(core, 0, summed, across, target, 0)


def final_kernel(core, mine, even, odd, target, ready, sems):
    parts = sems.shape[0]
    width = mine.shape[1] // parts
    copies = []
    for i in range(parts):
        lanes = pl.ds(i * width, width)

        @pl.when(core[0] == 0)
        def _():
            ready[:, lanes] = mine[:, lanes] + even[:, lanes].astype(jnp.float32)

        @pl.when(core[0] != 0)
        def _():
            ready[:, lanes] = mine[:, lanes] + odd[:, lanes].astype(jnp.float32)

        copies.append(pltpu.make_async_copy(ready.at[:, lanes], target.at[:, lanes], sems.at[i]))
        copies[-1].start()
    for copy in copies:
        copy.wait()


def call(kernel, outs, specs, args, out_specs=VMEM, **more):
    return pl.pallas_call(
        kernel,
        out_shape=outs,
        in_specs=specs,
        out_specs=out_specs,
        **more,
    )(*args)


LITTLE = pl.CostEstimate(flops=0, bytes_accessed=1024, transcendentals=0)


def in_hbm(array):
    return pltpu.with_memory_space_constraint(array, pltpu.HBM)


def params(mib):
    return pltpu.CompilerParams(vmem_limit_bytes=mib * 2**20)


def body(values, factor, cond, live):
    chains, row_count = values.shape
    blocks, rows, width = factor.shape
    slots = 3 * blocks + 2
    position = lax.axis_index(("curve", "rep"))
    core = lax.axis_index("rep").reshape(1)
    base = ((position - 2) * blocks).reshape(1)
    narrow = jax.ShapeDtypeStruct((chains, row_count), jnp.bfloat16)
    wide = jax.ShapeDtypeStruct((chains, row_count), jnp.float32)
    window_shape = jax.ShapeDtypeStruct((slots, chains, LANES), jnp.bfloat16)
    total_shape = jax.ShapeDtypeStruct((slots, chains // 2, LANES), jnp.float32)

    group_shape = (blocks // GROUP, GROUP * chains, GROUP * BS)

    two_odd = to_next_chip(values, 1)
    again = call(
        again_kernel,
        narrow,
        [HBM, SMEM, SMEM],
        (in_hbm(values), base, core),
        scratch_shapes=[pltpu.SemaphoreType.DMA],
        compiler_params=params(4),
        cost_estimate=LITTLE,
    )
    two_even = to_next_chip(again, 0)
    window, total, own_map, near_map, own_part = call(
        setup_kernel,
        (
            window_shape,
            total_shape,
            jax.ShapeDtypeStruct((blocks, rows, BS), factor.dtype),
            jax.ShapeDtypeStruct((blocks, rows, width - BS), factor.dtype),
            jax.ShapeDtypeStruct(group_shape, jnp.float32),
        ),
        [VMEM, HBM],
        (again, in_hbm(jnp.transpose(factor, (1, 2, 0)))),
        out_specs=(VMEM,) * 5,
        scratch_shapes=[
            pltpu.VMEM((PIECES, rows // PIECES, width, blocks), factor.dtype),
            pltpu.SemaphoreType.DMA((PIECES,)),
        ],
        compiler_params=params(SETUP_MIB),
        cost_estimate=pl.CostEstimate(flops=0, bytes_accessed=14 * 2**20, transcendentals=0),
    )
    payload = call(
        payload_kernel,
        narrow,
        [SMEM, VMEM, VMEM, VMEM],
        (core, again, two_odd, near_map),
        compiler_params=params(4), cost_estimate=LITTLE,
    )
    one = swap(payload)
    to_one, _, total, residuals = call(
        main_kernel,
        (wide, window_shape, total_shape, jax.ShapeDtypeStruct(group_shape, jnp.bfloat16)),
        [SMEM] * 4 + [VMEM] * 7,
        (core, base, jnp.transpose(cond), live, one, two_even, two_odd, window, total, near_map, own_part),
        out_specs=(VMEM,) * 4,
        scratch_shapes=[
            pltpu.SMEM((blocks * KN,), jnp.int32),
        ],
        input_output_aliases={7: 1, 8: 2},
        compiler_params=params(12),
        cost_estimate=pl.CostEstimate(
            flops=16 * blocks * rows * width * chains,
            bytes_accessed=8 * 2**20,
            transcendentals=0,
        ),
    )
    across = swap(to_one)
    to_two = call(two_kernel, narrow, [VMEM], (total,), compiler_params=params(4), cost_estimate=LITTLE)
    back = from_next_chip(to_two, 0)
    joint = call(
        joint_kernel,
        narrow,
        [SMEM, VMEM, VMEM],
        (core, total, across),
        compiler_params=params(4),
        cost_estimate=LITTLE,
    )
    joint = from_next_chip(joint, 1)
    mine = call(
        mine_kernel,
        wide,
        [SMEM, VMEM, VMEM, VMEM, VMEM],
        (core, total, across, residuals, own_map),
        scratch_shapes=[pltpu.VMEM((blocks, chains // 2, LANES), jnp.float32)],
        compiler_params=params(8),
        cost_estimate=LITTLE,
    )
    return call(
        final_kernel,
        wide,
        [SMEM, VMEM, VMEM, VMEM],
        (core, mine, back, joint),
        out_specs=HBM,
        scratch_shapes=[
            pltpu.VMEM((chains, row_count), jnp.float32),
            pltpu.SemaphoreType.DMA((PIECES,)),
        ],
        compiler_params=params(8),
    )


def solution(mesh):
    placed = (
        P("chain", ("region", "curve", "rep")),
        P(("region", "curve", "rep"), None, None),
        P(("region", "curve", "rep"), None),
        P(("region", "curve", "rep")),
    )
    return jax.shard_map(
        body,
        mesh=mesh,
        in_specs=placed,
        out_specs=P("chain", ("region", "curve", "rep")),
        check_vma=False,
    )
```

```python
import jax
import jax.numpy as jnp
from jax import lax
from jax.experimental import pallas as pl
from jax.experimental.pallas import tpu as pltpu
from jax.sharding import PartitionSpec as P

BS = 64
KN = 4
LANES = 128
GROUP = 4
LAG = 4
PIECES = 4
SETUP_MIB = 12

VMEM = pl.BlockSpec(memory_space=pltpu.VMEM)
SMEM = pl.BlockSpec(memory_space=pltpu.SMEM)
HBM = pl.BlockSpec(memory_space=pltpu.HBM)


def to_next_chip(block, core):
    size = lax.axis_size("curve")
    return lax.ppermute(
        block, ("curve", "rep"), [(2 * z + core, 2 * z + 2 + core) for z in range(size - 1)]
    )


def from_next_chip(block, core):
    size = lax.axis_size("curve")
    return lax.ppermute(
        block, ("curve", "rep"), [(2 * z + 2 + core, 2 * z + core) for z in range(size - 1)]
    )


def swap(block):
    return lax.ppermute(block, "rep", [(0, 1), (1, 0)])


def half_roll(tile):
    return pltpu.roll(tile, BS, tile.ndim - 1)


def lane_tile(t):
    return pl.ds(pl.multiple_of(t * LANES, LANES), LANES)


def low_lanes(rows):
    return lax.broadcasted_iota(jnp.int32, (rows, LANES), 1) < BS


def cross(low, first, second):
    kept = jnp.where(low, first, second)
    moved = half_roll(jnp.where(low, second, first))
    return jnp.where(low, kept, moved), jnp.where(low, moved, kept)


def spread(source, window, first_block):
    def step(t, carry):
        tile = source[:, lane_tile(t)]
        window[first_block + 2 * t] = tile
        window[first_block + 2 * t + 1] = half_roll(tile.astype(jnp.float32)).astype(tile.dtype)
        return carry

    lax.fori_loop(0, source.shape[1] // LANES, step, 0, unroll=64)


def collect(total, first_block, target):
    low = low_lanes(total.shape[1])

    def step(t, carry):
        even = first_block + 2 * t
        upper, lower = cross(low, total[even], total[even + 1])
        tile = jnp.concatenate([upper, lower], axis=0).astype(target.dtype)
        target[:, lane_tile(t)] = tile
        return carry

    lax.fori_loop(0, target.shape[1] // LANES, step, 0, unroll=64)


def again_kernel(own, again, sem):
    copy = pltpu.make_async_copy(own, again, sem)
    copy.start()
    copy.wait()


def setup_kernel(own, flipped, window, total, own_map, near_map, own_part, staged, sems):
    pieces, rows = staged.shape[:2]
    blocks = near_map.shape[0]
    half = total.shape[1]
    copies = [
        pltpu.make_async_copy(flipped.at[pl.ds(i * rows, rows)], staged.at[i], sems.at[i])
        for i in range(pieces)
    ]
    for copy in copies:
        copy.start()
    spread(own, window, 2 * blocks)
    window[pl.ds(3 * blocks, 2)] = jnp.zeros((2,) + window.shape[1:], window.dtype)

    def clear(i, carry):
        total[pl.ds(i * 8, 8)] = jnp.zeros((8, half, LANES), jnp.float32)
        return carry

    lax.fori_loop(0, 3 * blocks // 8, clear, 0, unroll=4)
    total[3 * blocks] = jnp.zeros((half, LANES), jnp.float32)
    for i, copy in enumerate(copies):
        copy.wait()
        part = pl.ds(i * rows, rows)
        own_map[:, part, :] = jnp.transpose(staged[i, :, :BS], (2, 0, 1))
        near_map[:, part, :] = jnp.transpose(staged[i, :, BS:], (2, 0, 1))

    def start(q, carry):
        first = q * GROUP
        mine = [window[2 * blocks + first + b][:, :BS] for b in range(GROUP)]
        maps = own_map[pl.ds(first, GROUP)].reshape(GROUP * BS, BS)
        own_part[q] = lax.dot_general(
            jnp.concatenate(mine, axis=0),
            maps,
            (((1,), (1,)), ((), ())),
            preferred_element_type=jnp.float32,
        )
        return carry

    lax.fori_loop(0, blocks // GROUP, start, 0, unroll=8)


def payload_kernel(own, arrived, factor, target):
    core = lax.axis_index("rep")

    @pl.when(core == 0)
    def _():
        target[...] = own[...]

    @pl.when(core != 0)
    def _():
        target[...] = arrived[...]


def main_kernel(
    cond, live, one, two_even, two_odd, window_in, total_in, near_map, own_part,
    out_one, window, total, residuals, index,
):
    chains = window.shape[1]
    half = chains // 2
    blocks = near_map.shape[0]

    core = lax.axis_index("rep")
    base = (lax.axis_index("curve") * 2 + core - 2) * blocks
    spread(one, window, blocks)

    @pl.when(core == 0)
    def _():
        spread(two_even, window, 0)

    @pl.when(core != 0)
    def _():
        spread(two_odd, window, 0)

    low = low_lanes(chains)
    half_low = low_lanes(half)
    shape = (GROUP * chains, GROUP * BS)
    row_block = lax.broadcasted_iota(jnp.int32, shape, 0) // chains
    lane_block = lax.broadcasted_iota(jnp.int32, shape, 1) // BS
    diagonal = row_block == lane_block
    live_count = live[0]

    def pull(q):
        first = q * GROUP
        stacked = []
        for b in range(GROUP):
            g = first + b
            at = []
            for k in range(KN):
                place = cond[k, g]
                place = jnp.where(place >= 0, place - base, 3 * blocks)
                index[g * KN + k] = place
                at.append(place)
            stacked.append(
                jnp.concatenate(
                    [
                        jnp.where(low, window[at[0]], window[at[1] ^ 1]),
                        jnp.where(low, window[at[2]], window[at[3] ^ 1]),
                    ],
                    axis=1,
                )
            )
        stacked = jnp.concatenate(stacked, axis=0)
        maps = near_map[pl.ds(first, GROUP)].reshape(GROUP * BS, BS * KN)
        residual = lax.dot_general(
            stacked, maps, (((1,), (1,)), ((), ())), preferred_element_type=jnp.float32
        )
        residual = residual + own_part[q]
        kept = diagonal & (lane_block < live_count - first)
        residuals[q] = jnp.where(kept, -residual, 0.0).astype(jnp.bfloat16)

    def push(q):
        first = q * GROUP
        maps = near_map[pl.ds(first, GROUP)].reshape(GROUP * BS, BS * KN)
        terms = jnp.dot(residuals[q], maps, preferred_element_type=jnp.float32)
        for b in range(GROUP):
            g = first + b
            at = [index[g * KN + k] for k in range(KN)]
            a = terms[b * chains : b * chains + half]
            z = terms[b * chains + half : (b + 1) * chains]
            t0, t1 = cross(half_low, a[:, :LANES], z[:, :LANES])
            t2, t3 = cross(half_low, a[:, LANES:], z[:, LANES:])
            old = [total[at[k]] for k in range(KN)]
            for k, term in enumerate((t0, t1, t2, t3)):
                total[at[k]] = old[k] + term

    groups = blocks // GROUP
    for q in range(groups + LAG):
        if q < groups:
            pull(q)
        if q >= LAG:
            push(q - LAG)
    collect(total, blocks, out_one)


def add_across(keeper, total, across, target, first_block):
    low = low_lanes(total.shape[1])
    share = jnp.where(lax.axis_index("rep") == keeper, 1.0, 0.0)

    def step(t, carry):
        even = first_block + 2 * t
        upper, lower = cross(low, total[even], total[even + 1])
        tile = jnp.concatenate([upper, lower], axis=0)
        tile = tile + share * across[:, lane_tile(t)].astype(jnp.float32)
        target[:, lane_tile(t)] = tile.astype(target.dtype)
        return carry

    lax.fori_loop(0, target.shape[1] // LANES, step, 0, unroll=64)


def two_kernel(total, target):
    collect(total, 0, target)


def joint_kernel(total, across, target):
    add_across(1, total, across, target, 0)


def mine_kernel(total, across, residuals, own_map, target, summed):
    blocks = own_map.shape[0]
    chains = target.shape[0]
    half = chains // 2

    def step(q, carry):
        first = q * GROUP
        maps = own_map[pl.ds(first, GROUP)].reshape(GROUP * BS, BS)
        terms = jnp.dot(residuals[q], maps, preferred_element_type=jnp.float32)
        for b in range(GROUP):
            a = terms[b * chains : b * chains + half]
            z = terms[b * chains + half : (b + 1) * chains]
            packed = jnp.concatenate([a, z], axis=1)
            summed[first + b] = total[2 * blocks + first + b] + packed
        return carry

    lax.fori_loop(0, blocks // GROUP, step, 0, unroll=4)
    add_across(0, summed, across, target, 0)


def final_kernel(mine, even, odd, target, ready, sems):
    core = lax.axis_index("rep")
    parts = sems.shape[0]
    width = mine.shape[1] // parts
    copies = []
    for i in range(parts):
        lanes = pl.ds(i * width, width)

        @pl.when(core == 0)
        def _():
            ready[:, lanes] = mine[:, lanes] + even[:, lanes].astype(jnp.float32)

        @pl.when(core != 0)
        def _():
            ready[:, lanes] = mine[:, lanes] + odd[:, lanes].astype(jnp.float32)

        copies.append(pltpu.make_async_copy(ready.at[:, lanes], target.at[:, lanes], sems.at[i]))
        copies[-1].start()
    for copy in copies:
        copy.wait()


def call(kernel, outs, specs, args, out_specs=VMEM, **more):
    return pl.pallas_call(
        kernel,
        out_shape=outs,
        in_specs=specs,
        out_specs=out_specs,
        **more,
    )(*args)


LITTLE = pl.CostEstimate(flops=0, bytes_accessed=1024, transcendentals=0)


def in_hbm(array):
    return pltpu.with_memory_space_constraint(array, pltpu.HBM)


def params(mib):
    return pltpu.CompilerParams(vmem_limit_bytes=mib * 2**20)


def body(values, factor, cond, live):
    chains, row_count = values.shape
    blocks, rows, width = factor.shape
    slots = 3 * blocks + 2
    narrow = jax.ShapeDtypeStruct((chains, row_count), jnp.bfloat16)
    wide = jax.ShapeDtypeStruct((chains, row_count), jnp.float32)
    window_shape = jax.ShapeDtypeStruct((slots, chains, LANES), jnp.bfloat16)
    total_shape = jax.ShapeDtypeStruct((slots, chains // 2, LANES), jnp.float32)

    group_shape = (blocks // GROUP, GROUP * chains, GROUP * BS)

    two_odd = to_next_chip(values, 1)
    again = call(
        again_kernel,
        narrow,
        [HBM],
        (in_hbm(values),),
        scratch_shapes=[pltpu.SemaphoreType.DMA],
        compiler_params=params(4),
        cost_estimate=LITTLE,
    )
    two_even = to_next_chip(again, 0)
    window, total, own_map, near_map, own_part = call(
        setup_kernel,
        (
            window_shape,
            total_shape,
            jax.ShapeDtypeStruct((blocks, rows, BS), factor.dtype),
            jax.ShapeDtypeStruct((blocks, rows, width - BS), factor.dtype),
            jax.ShapeDtypeStruct(group_shape, jnp.float32),
        ),
        [VMEM, HBM],
        (again, in_hbm(jnp.transpose(factor, (1, 2, 0)))),
        out_specs=(VMEM,) * 5,
        scratch_shapes=[
            pltpu.VMEM((PIECES, rows // PIECES, width, blocks), factor.dtype),
            pltpu.SemaphoreType.DMA((PIECES,)),
        ],
        compiler_params=params(SETUP_MIB),
        cost_estimate=pl.CostEstimate(flops=0, bytes_accessed=14 * 2**20, transcendentals=0),
    )
    payload = call(
        payload_kernel,
        narrow,
        [VMEM, VMEM, VMEM],
        (again, two_odd, near_map),
        compiler_params=params(4), cost_estimate=LITTLE,
    )
    one = swap(payload)
    to_one, _, total, residuals = call(
        main_kernel,
        (wide, window_shape, total_shape, jax.ShapeDtypeStruct(group_shape, jnp.bfloat16)),
        [SMEM] * 2 + [VMEM] * 7,
        (jnp.transpose(cond), live, one, two_even, two_odd, window, total, near_map, own_part),
        out_specs=(VMEM,) * 4,
        scratch_shapes=[
            pltpu.SMEM((blocks * KN,), jnp.int32),
        ],
        input_output_aliases={5: 1, 6: 2},
        compiler_params=params(12),
        cost_estimate=pl.CostEstimate(
            flops=16 * blocks * rows * width * chains,
            bytes_accessed=8 * 2**20,
            transcendentals=0,
        ),
    )
    across = swap(to_one)
    to_two = call(two_kernel, narrow, [VMEM], (total,), compiler_params=params(4), cost_estimate=LITTLE)
    back = from_next_chip(to_two, 0)
    joint = call(
        joint_kernel,
        narrow,
        [VMEM, VMEM],
        (total, across),
        compiler_params=params(4),
        cost_estimate=LITTLE,
    )
    joint = from_next_chip(joint, 1)
    mine = call(
        mine_kernel,
        wide,
        [VMEM, VMEM, VMEM, VMEM],
        (total, across, residuals, own_map),
        scratch_shapes=[pltpu.VMEM((blocks, chains // 2, LANES), jnp.float32)],
        compiler_params=params(8),
        cost_estimate=LITTLE,
    )
    return call(
        final_kernel,
        wide,
        [VMEM, VMEM, VMEM],
        (mine, back, joint),
        out_specs=HBM,
        scratch_shapes=[
            pltpu.VMEM((chains, row_count), jnp.float32),
            pltpu.SemaphoreType.DMA((PIECES,)),
        ],
        compiler_params=params(8),
    )


def solution(mesh):
    placed = (
        P("chain", ("region", "curve", "rep")),
        P(("region", "curve", "rep"), None, None),
        P(("region", "curve", "rep"), None),
        P(("region", "curve", "rep")),
    )
    return jax.shard_map(
        body,
        mesh=mesh,
        in_specs=placed,
        out_specs=P("chain", ("region", "curve", "rep")),
        check_vma=False,
    )
```

```python
import jax
import jax.numpy as jnp
from jax import lax
from jax.experimental import pallas as pl
from jax.experimental.pallas import tpu as pltpu
from jax.sharding import PartitionSpec as P

BS = 64
KN = 4
LANES = 128
GROUP = 4
LAG = 4
PIECES = 4
SETUP_MIB = 12

VMEM = pl.BlockSpec(memory_space=pltpu.VMEM)
SMEM = pl.BlockSpec(memory_space=pltpu.SMEM)
HBM = pl.BlockSpec(memory_space=pltpu.HBM)


def to_next_chip(block, core):
    size = lax.axis_size("curve")
    return lax.ppermute(
        block, ("curve", "rep"), [(2 * z + core, 2 * z + 2 + core) for z in range(size - 1)]
    )


def from_next_chip(block, core):
    size = lax.axis_size("curve")
    return lax.ppermute(
        block, ("curve", "rep"), [(2 * z + 2 + core, 2 * z + core) for z in range(size - 1)]
    )


def swap(block):
    return lax.ppermute(block, "rep", [(0, 1), (1, 0)])


def half_roll(tile):
    return pltpu.roll(tile, BS, tile.ndim - 1)


def lane_tile(t):
    return pl.ds(pl.multiple_of(t * LANES, LANES), LANES)


def low_lanes(rows):
    return lax.broadcasted_iota(jnp.int32, (rows, LANES), 1) < BS


def cross(low, first, second):
    kept = jnp.where(low, first, second)
    moved = half_roll(jnp.where(low, second, first))
    return jnp.where(low, kept, moved), jnp.where(low, moved, kept)


def spread(source, window, first_block):
    def step(t, carry):
        tile = source[:, lane_tile(t)]
        window[first_block + 2 * t] = tile
        window[first_block + 2 * t + 1] = half_roll(tile.astype(jnp.float32)).astype(tile.dtype)
        return carry

    lax.fori_loop(0, source.shape[1] // LANES, step, 0, unroll=64)


def collect(total, first_block, target):
    low = low_lanes(total.shape[1])

    def step(t, carry):
        even = first_block + 2 * t
        upper, lower = cross(low, total[even], total[even + 1])
        tile = jnp.concatenate([upper, lower], axis=0).astype(target.dtype)
        target[:, lane_tile(t)] = tile
        return carry

    lax.fori_loop(0, target.shape[1] // LANES, step, 0, unroll=64)


def again_kernel(own, again, sem):
    copy = pltpu.make_async_copy(own, again, sem)
    copy.start()
    copy.wait()


def setup_kernel(own, flipped, window, total, own_map, near_map, own_part, staged, sems):
    pieces, rows = staged.shape[:2]
    blocks = near_map.shape[0]
    half = total.shape[1]
    copies = [
        pltpu.make_async_copy(flipped.at[pl.ds(i * rows, rows)], staged.at[i], sems.at[i])
        for i in range(pieces)
    ]
    for copy in copies:
        copy.start()
    spread(own, window, 2 * blocks)
    window[pl.ds(3 * blocks, 2)] = jnp.zeros((2,) + window.shape[1:], window.dtype)

    def clear(i, carry):
        total[pl.ds(i * 8, 8)] = jnp.zeros((8, half, LANES), jnp.float32)
        return carry

    lax.fori_loop(0, 3 * blocks // 8, clear, 0, unroll=4)
    total[3 * blocks] = jnp.zeros((half, LANES), jnp.float32)
    for i, copy in enumerate(copies):
        copy.wait()
        part = pl.ds(i * rows, rows)
        own_map[:, part, :] = jnp.transpose(staged[i, :, :BS], (2, 0, 1))
        near_map[:, part, :] = jnp.transpose(staged[i, :, BS:], (2, 0, 1))

    def start(q, carry):
        first = q * GROUP
        mine = [window[2 * blocks + first + b][:, :BS] for b in range(GROUP)]
        maps = own_map[pl.ds(first, GROUP)].reshape(GROUP * BS, BS)
        own_part[q] = lax.dot_general(
            jnp.concatenate(mine, axis=0),
            maps,
            (((1,), (1,)), ((), ())),
            preferred_element_type=jnp.float32,
        )
        return carry

    lax.fori_loop(0, blocks // GROUP, start, 0, unroll=8)


def payload_kernel(own, arrived, factor, target):
    core = lax.axis_index("rep")

    @pl.when(core == 0)
    def _():
        target[...] = own[...]

    @pl.when(core != 0)
    def _():
        target[...] = arrived[...]


def main_kernel(
    cond_in, live, one, two_even, two_odd, window_in, total_in, near_map, own_part,
    out_one, window, total, residuals, index, cond, sem,
):
    chains = window.shape[1]
    half = chains // 2
    blocks = near_map.shape[0]

    core = lax.axis_index("rep")
    base = (lax.axis_index("curve") * 2 + core - 2) * blocks
    fetch = pltpu.make_async_copy(cond_in, cond, sem)
    fetch.start()
    spread(one, window, blocks)

    @pl.when(core == 0)
    def _():
        spread(two_even, window, 0)

    @pl.when(core != 0)
    def _():
        spread(two_odd, window, 0)

    low = low_lanes(chains)
    half_low = low_lanes(half)
    shape = (GROUP * chains, GROUP * BS)
    row_block = lax.broadcasted_iota(jnp.int32, shape, 0) // chains
    lane_block = lax.broadcasted_iota(jnp.int32, shape, 1) // BS
    diagonal = row_block == lane_block
    live_count = live[0]

    def pull(q):
        first = q * GROUP
        stacked = []
        for b in range(GROUP):
            g = first + b
            at = []
            for k in range(KN):
                place = cond[k, g]
                place = jnp.where(place >= 0, place - base, 3 * blocks)
                index[g * KN + k] = place
                at.append(place)
            stacked.append(
                jnp.concatenate(
                    [
                        jnp.where(low, window[at[0]], window[at[1] ^ 1]),
                        jnp.where(low, window[at[2]], window[at[3] ^ 1]),
                    ],
                    axis=1,
                )
            )
        stacked = jnp.concatenate(stacked, axis=0)
        maps = near_map[pl.ds(first, GROUP)].reshape(GROUP * BS, BS * KN)
        residual = lax.dot_general(
            stacked, maps, (((1,), (1,)), ((), ())), preferred_element_type=jnp.float32
        )
        residual = residual + own_part[q]
        kept = diagonal & (lane_block < live_count - first)
        residuals[q] = jnp.where(kept, -residual, 0.0).astype(jnp.bfloat16)

    def push(q):
        first = q * GROUP
        maps = near_map[pl.ds(first, GROUP)].reshape(GROUP * BS, BS * KN)
        terms = jnp.dot(residuals[q], maps, preferred_element_type=jnp.float32)
        for b in range(GROUP):
            g = first + b
            at = [index[g * KN + k] for k in range(KN)]
            a = terms[b * chains : b * chains + half]
            z = terms[b * chains + half : (b + 1) * chains]
            t0, t1 = cross(half_low, a[:, :LANES], z[:, :LANES])
            t2, t3 = cross(half_low, a[:, LANES:], z[:, LANES:])
            old = [total[at[k]] for k in range(KN)]
            for k, term in enumerate((t0, t1, t2, t3)):
                total[at[k]] = old[k] + term

    fetch.wait()
    groups = blocks // GROUP
    for q in range(groups + LAG):
        if q < groups:
            pull(q)
        if q >= LAG:
            push(q - LAG)
    collect(total, blocks, out_one)


def add_across(keeper, total, across, target, first_block):
    low = low_lanes(total.shape[1])
    share = jnp.where(lax.axis_index("rep") == keeper, 1.0, 0.0)

    def step(t, carry):
        even = first_block + 2 * t
        upper, lower = cross(low, total[even], total[even + 1])
        tile = jnp.concatenate([upper, lower], axis=0)
        tile = tile + share * across[:, lane_tile(t)].astype(jnp.float32)
        target[:, lane_tile(t)] = tile.astype(target.dtype)
        return carry

    lax.fori_loop(0, target.shape[1] // LANES, step, 0, unroll=64)


def two_kernel(total, target):
    collect(total, 0, target)


def joint_kernel(total, across, target):
    add_across(1, total, across, target, 0)


def mine_kernel(total, across, residuals, own_map, target, summed):
    blocks = own_map.shape[0]
    chains = target.shape[0]
    half = chains // 2

    def step(q, carry):
        first = q * GROUP
        maps = own_map[pl.ds(first, GROUP)].reshape(GROUP * BS, BS)
        terms = jnp.dot(residuals[q], maps, preferred_element_type=jnp.float32)
        for b in range(GROUP):
            a = terms[b * chains : b * chains + half]
            z = terms[b * chains + half : (b + 1) * chains]
            packed = jnp.concatenate([a, z], axis=1)
            summed[first + b] = total[2 * blocks + first + b] + packed
        return carry

    lax.fori_loop(0, blocks // GROUP, step, 0, unroll=4)
    add_across(0, summed, across, target, 0)


def final_kernel(mine, even, odd, target, ready, sems):
    core = lax.axis_index("rep")
    parts = sems.shape[0]
    width = mine.shape[1] // parts
    copies = []
    for i in range(parts):
        lanes = pl.ds(i * width, width)

        @pl.when(core == 0)
        def _():
            ready[:, lanes] = mine[:, lanes] + even[:, lanes].astype(jnp.float32)

        @pl.when(core != 0)
        def _():
            ready[:, lanes] = mine[:, lanes] + odd[:, lanes].astype(jnp.float32)

        copies.append(pltpu.make_async_copy(ready.at[:, lanes], target.at[:, lanes], sems.at[i]))
        copies[-1].start()
    for copy in copies:
        copy.wait()


def call(kernel, outs, specs, args, out_specs=VMEM, **more):
    return pl.pallas_call(
        kernel,
        out_shape=outs,
        in_specs=specs,
        out_specs=out_specs,
        **more,
    )(*args)


LITTLE = pl.CostEstimate(flops=0, bytes_accessed=1024, transcendentals=0)


def in_hbm(array):
    return pltpu.with_memory_space_constraint(array, pltpu.HBM)


def params(mib):
    return pltpu.CompilerParams(vmem_limit_bytes=mib * 2**20)


def body(values, factor, cond, live):
    chains, row_count = values.shape
    blocks, rows, width = factor.shape
    slots = 3 * blocks + 2
    narrow = jax.ShapeDtypeStruct((chains, row_count), jnp.bfloat16)
    wide = jax.ShapeDtypeStruct((chains, row_count), jnp.float32)
    window_shape = jax.ShapeDtypeStruct((slots, chains, LANES), jnp.bfloat16)
    total_shape = jax.ShapeDtypeStruct((slots, chains // 2, LANES), jnp.float32)

    group_shape = (blocks // GROUP, GROUP * chains, GROUP * BS)

    two_odd = to_next_chip(values, 1)
    again = call(
        again_kernel,
        narrow,
        [HBM],
        (in_hbm(values),),
        scratch_shapes=[pltpu.SemaphoreType.DMA],
        compiler_params=params(4),
        cost_estimate=LITTLE,
    )
    two_even = to_next_chip(again, 0)
    window, total, own_map, near_map, own_part = call(
        setup_kernel,
        (
            window_shape,
            total_shape,
            jax.ShapeDtypeStruct((blocks, rows, BS), factor.dtype),
            jax.ShapeDtypeStruct((blocks, rows, width - BS), factor.dtype),
            jax.ShapeDtypeStruct(group_shape, jnp.float32),
        ),
        [VMEM, HBM],
        (again, in_hbm(jnp.transpose(factor, (1, 2, 0)))),
        out_specs=(VMEM,) * 5,
        scratch_shapes=[
            pltpu.VMEM((PIECES, rows // PIECES, width, blocks), factor.dtype),
            pltpu.SemaphoreType.DMA((PIECES,)),
        ],
        compiler_params=params(SETUP_MIB),
        cost_estimate=pl.CostEstimate(flops=0, bytes_accessed=14 * 2**20, transcendentals=0),
    )
    payload = call(
        payload_kernel,
        narrow,
        [VMEM, VMEM, VMEM],
        (again, two_odd, near_map),
        compiler_params=params(4), cost_estimate=LITTLE,
    )
    one = swap(payload)
    to_one, _, total, residuals = call(
        main_kernel,
        (wide, window_shape, total_shape, jax.ShapeDtypeStruct(group_shape, jnp.bfloat16)),
        [HBM, SMEM] + [VMEM] * 7,
        (in_hbm(jnp.transpose(cond)), live, one, two_even, two_odd, window, total, near_map, own_part),
        out_specs=(VMEM,) * 4,
        scratch_shapes=[
            pltpu.SMEM((blocks * KN,), jnp.int32),
            pltpu.SMEM((KN, blocks), jnp.int32),
            pltpu.SemaphoreType.DMA,
        ],
        input_output_aliases={5: 1, 6: 2},
        compiler_params=params(12),
        cost_estimate=pl.CostEstimate(
            flops=16 * blocks * rows * width * chains,
            bytes_accessed=8 * 2**20,
            transcendentals=0,
        ),
    )
    across = swap(to_one)
    to_two = call(two_kernel, narrow, [VMEM], (total,), compiler_params=params(4), cost_estimate=LITTLE)
    back = from_next_chip(to_two, 0)
    joint = call(
        joint_kernel,
        narrow,
        [VMEM, VMEM],
        (total, across),
        compiler_params=params(4),
        cost_estimate=LITTLE,
    )
    joint = from_next_chip(joint, 1)
    mine = call(
        mine_kernel,
        wide,
        [VMEM, VMEM, VMEM, VMEM],
        (total, across, residuals, own_map),
        scratch_shapes=[pltpu.VMEM((blocks, chains // 2, LANES), jnp.float32)],
        compiler_params=params(8),
        cost_estimate=LITTLE,
    )
    return call(
        final_kernel,
        wide,
        [VMEM, VMEM, VMEM],
        (mine, back, joint),
        out_specs=HBM,
        scratch_shapes=[
            pltpu.VMEM((chains, row_count), jnp.float32),
            pltpu.SemaphoreType.DMA((2 * PIECES,)),
        ],
        compiler_params=params(8),
    )


def solution(mesh):
    placed = (
        P("chain", ("region", "curve", "rep")),
        P(("region", "curve", "rep"), None, None),
        P(("region", "curve", "rep"), None),
        P(("region", "curve", "rep")),
    )
    return jax.shard_map(
        body,
        mesh=mesh,
        in_specs=placed,
        out_specs=P("chain", ("region", "curve", "rep")),
        check_vma=False,
    )
```
